128 devices in a mesh: gx: 8 (over x_hi, y), gy: 16 (over z, x_lo, core).
Axes of the slice: x: 4 (x_hi: 2, x_lo: 2; x = x_hi * 2 + x_lo), y: 4, z: 4, core: 2. Of those that a mesh axis runs over, the one named last changes fastest.
Arguments:
- charges: bfloat16 [32, 64, 16, 256], P('gx', 'gy'), may hold values from -6 to 6
- basis: bfloat16 [32, 64, 64, 256], P('gx', 'gy'), may hold values from -0.375 to 0.375
- near_blocks: bfloat16 [32, 64, 8, 256, 256], P('gx', 'gy'), may hold values from -0.125 to 0.125
- near_list: int32 [32, 64, 8], P('gx', 'gy'), may hold values from 0 to 8, as said below
- far_list: int32 [32, 64, 8], P('gx', 'gy'), may hold values from 0 to 15, as said below
- coupling: bfloat16 [32, 64, 64, 512], P('gx', 'gy'), may hold values from -0.25 to 0.25
- transfer: bfloat16 [32, 64, 64, 64], P('gx', 'gy'), may hold values from -0.375 to 0.375
- coarse_transfer: bfloat16 [8, 16, 64, 64], P('gx', 'gy'), may hold values from -0.375 to 0.375
- coarse_group: int32 [128], replicated, may hold values from 0 to 15, as said below
- coarse_pattern: int32 [16, 16], replicated, may hold values 0 or 1
- coarse_coupling: bfloat16 [16, 64, 1024], replicated, may hold values from -0.1875 to 0.1875
Outputs:
- potential: bfloat16 [32, 64, 16, 256], P('gx', 'gy')
The draws below stay inside these ranges and needn't reach their ends.
Inputs may be any that keep to these rules, and one draw needn't show every extreme that they name: `near_list`: the 8 entries of one leaf are distinct. `far_list`: the 8 entries of one leaf are distinct. `coarse_group`: every coarse cluster has exactly 8 device clusters.
All inputs are finite; a program needn't handle non-finite values.
Results may differ from the reference program's by a relative error of at most 0.015.
Values may be sent and summed in bfloat16 or wider, within the bound.
A program may use at most 64 MiB of HBM per device.

```python
import jax
import jax.numpy as jnp
from jax import lax

K = 64
PT = 256
NV = 16
NNEAR = 8
NINT = 8
GROUP = 8
LX = 4
LY = 4
NLX = 32
NLY = 64
NCLUS = 128
NCOARSE = 16
N_GX = 8
N_GY = 16


def distinct_picks(key, options_total, picks):
    scores = jax.random.randint(key, (NLX, NLY, options_total), 0, 1 << 20) * options_total + jnp.arange(options_total, dtype=jnp.int32)
    ordered = jnp.argsort(scores, axis=-1)
    return ordered[:, :, :picks].astype(jnp.int32)


def draw_near_list(key, part):
    key = jax.random.fold_in(key, 11)
    return distinct_picks(key, 9, NNEAR)


def draw_far_list(key, part):
    key = jax.random.fold_in(key, 12)
    return distinct_picks(key, 16, NINT)


def draw_coarse_group(key, part):
    key = jax.random.fold_in(key, 13)
    return (jax.random.permutation(key, NCLUS) // GROUP).astype(jnp.int32)


def with_ends(drawn, rng, low, top_value):
    place = [jax.random.randint(jax.random.fold_in(rng, axis), (), 0, length) for axis, length in enumerate(drawn.shape)]
    longest = drawn.shape.index(max(drawn.shape))
    next_to = place[:longest] + [(place[longest] + 1) % drawn.shape[longest]] + place[longest + 1:]
    return drawn.at[tuple(place)].set(low).at[tuple(next_to)].set(top_value)


def block_levels(rng, extent, shards, smallest, largest):
    gain, own = 1.0, jax.random.fold_in(rng, 6)
    for axis_at, blocks in shards:
        draws = jnp.exp(jax.random.uniform(jax.random.fold_in(own, axis_at), (blocks,), jnp.float32, smallest / len(shards), largest / len(shards)))
        gain = gain * jnp.repeat(draws, extent[axis_at] // blocks).reshape([-1 if axis == axis_at else 1 for axis in range(len(extent))])
    return gain


def bell_draw(own_key, extent, spread, bound, shards=(), kind=jnp.bfloat16):
    values = jax.random.normal(own_key, extent, jnp.float32) * spread
    if len(shards) > 0:
        values = block_levels(own_key, extent, shards, -0.22, 0.18) * values
    return jnp.clip(values, min=-bound, max=bound).astype(kind)


def setup_inputs(seed: int = 0) -> dict:
    streams_of = jax.random.split(jax.random.key(seed), 12)
    charges = bell_draw(streams_of[0], (NLX, NLY, NV, PT), 1.0, 6.0, ((0, 8), (1, 16)))
    basis = bell_draw(streams_of[1], (NLX, NLY, K, PT), PT ** -0.5, 0.375, ((0, 8), (1, 16)))
    near_blocks = bell_draw(streams_of[2], (NLX, NLY, NNEAR, PT, PT), (NNEAR * PT) ** -0.5, 0.125, ((0, 8), (1, 16)))
    near_list = draw_near_list(jax.random.fold_in(streams_of[11], 71), 0)
    far_list = draw_far_list(jax.random.fold_in(streams_of[11], 71), 0)
    coupling = bell_draw(streams_of[5], (NLX, NLY, K, NINT * K), (NINT * K) ** -0.5, 0.25, ((0, 8), (1, 16)))
    transfer = bell_draw(streams_of[6], (NLX, NLY, K, K), (K * LX) ** -0.5, 0.375, ((0, 8), (1, 16)))
    coarse_transfer = bell_draw(streams_of[7], (N_GX, N_GY, K, K), (K * LY) ** -0.5, 0.375, ((0, 8), (1, 16)))
    coarse_group = draw_coarse_group(jax.random.fold_in(streams_of[11], 71), 0)
    coarse_pattern = with_ends((jax.random.randint(streams_of[9], (NCOARSE, NCOARSE), 0, 4) < 3).astype(jnp.int32), jax.random.fold_in(streams_of[9], 1), 0, 1)
    coarse_coupling = bell_draw(streams_of[10], (NCOARSE, K, NCOARSE * K), (NCOARSE * K) ** -0.5, 0.1875)
    return {"charges": charges, "basis": basis, "near_blocks": near_blocks, "near_list": near_list, "far_list": far_list, "coupling": coupling, "transfer": transfer, "coarse_transfer": coarse_transfer, "coarse_group": coarse_group, "coarse_pattern": coarse_pattern, "coarse_coupling": coarse_coupling}


cycle_offsets = [(shift_x, shift_y) for shift_x in range(-2, 3) for shift_y in range(-2, 3) if max(abs(shift_x), abs(shift_y)) == 2]
near_offsets = [(number // 3 - 1, number % 3 - 1) for number in range(9)]


def select(stacked, wanted):
    picked = jnp.zeros(stacked.shape[1:], stacked.dtype)
    for number in range(stacked.shape[0]):
        matches = (wanted == number).reshape(wanted.shape + (1,) * (stacked.ndim - 1 - wanted.ndim))
        picked = jnp.where(matches, stacked[number], picked)
    return picked


def rolled(values, offsets):
    return jnp.stack([jnp.roll(values, (-shift_x, -shift_y), axis=(0, 1)) for shift_x, shift_y in offsets])


def near_row(leaf_row):
    blocks, sources = leaf_row
    return jnp.einsum("bmpq,bmvq->bvp", blocks.astype(jnp.float32), sources.astype(jnp.float32))


def reference(charges, basis, near_blocks, near_list, far_list, coupling, transfer, coarse_transfer, coarse_group, coarse_pattern, coarse_coupling):
    leaf_coef = jnp.einsum("abkp,abvp->abkv", basis.astype(jnp.float32), charges.astype(jnp.float32)).astype(jnp.bfloat16)
    lifted = jnp.einsum("abkl,ablv->abkv", transfer.astype(jnp.float32), leaf_coef.astype(jnp.float32))
    cluster_coef = lifted.reshape(N_GX, LX, N_GY, LY, K, NV).sum(axis=(1, 3)).astype(jnp.bfloat16)
    coarse_term = jnp.einsum("xykl,xylv->xykv", coarse_transfer.astype(jnp.float32), cluster_coef.astype(jnp.float32)).reshape(NCLUS, K, NV)
    coarse_sum = jax.ops.segment_sum(coarse_term, coarse_group, NCOARSE)
    coarse_coef = coarse_sum.astype(jnp.bfloat16)
    weights = coarse_coupling.astype(jnp.float32).reshape(NCOARSE, K, NCOARSE, K) * coarse_pattern.astype(jnp.float32)[:, None, :, None]
    coarse_far = jnp.einsum("gkhl,hlv->gkv", weights, coarse_coef.astype(jnp.float32)).astype(jnp.bfloat16)
    group_far = coarse_far[coarse_group].reshape(N_GX, N_GY, K, NV)
    cluster_far = jnp.einsum("xylk,xylv->xykv", coarse_transfer.astype(jnp.float32), group_far.astype(jnp.float32)).astype(jnp.bfloat16)
    parent_far = jnp.repeat(jnp.repeat(cluster_far, LX, axis=0), LY, axis=1)
    lowered = jnp.einsum("ablk,ablv->abkv", transfer.astype(jnp.float32), parent_far.astype(jnp.float32))
    cycle_coef = rolled(leaf_coef, cycle_offsets)
    far_coef = jnp.stack([select(cycle_coef, far_list[:, :, column]) for column in range(NINT)], axis=2)
    coupled = jnp.einsum("abkc,abcv->abkv", coupling.astype(jnp.float32), far_coef.reshape(NLX, NLY, NINT * K, NV).astype(jnp.float32))
    leaf_far = (coupled + lowered).astype(jnp.bfloat16)
    far_part = jnp.einsum("abkp,abkv->abvp", basis.astype(jnp.float32), leaf_far.astype(jnp.float32))
    beside_all = rolled(charges, near_offsets)
    near_charges = jnp.stack([select(beside_all, near_list[:, :, column]) for column in range(NNEAR)], axis=2)
    near_part = lax.map(near_row, (near_blocks, near_charges))
    return (far_part + near_part).astype(jnp.bfloat16)
```

```python
import functools

import jax
import jax.numpy as jnp
from jax import lax
from jax.experimental import pallas as pl
from jax.experimental.pallas import tpu as pltpu
from jax.sharding import PartitionSpec as P

MESH = pl.DeviceIdType.MESH
NT = (((1,), (1,)), ((), ()))
NN = (((1,), (0,)), ((), ()))
bf16 = jnp.bfloat16
f32 = jnp.float32

SIDES = [(sx, sy) for sx in (-1, 0, 1) for sy in (-1, 0, 1) if (sx, sy) != (0, 0)]


def dot(left, right, dims):
    return lax.dot_general(left, right, dims, preferred_element_type=f32)


def strip(side, depth, count):
    if side == 0:
        return pl.ds(0, count), pl.ds(depth, count)
    if side > 0:
        return pl.ds(count - depth, depth), pl.ds(0, depth)
    return pl.ds(0, depth), pl.ds(count + depth, depth)


def kernel(
    n_gx,
    n_gy,
    charges,
    basis,
    near_blocks,
    near_list,
    far_list,
    coupling,
    transfer,
    coarse_transfer,
    coarse_group,
    coarse_pattern,
    coarse_coupling,
    out,
    charge_pad,
    basis_v,
    near_v,
    near_s,
    far_s,
    coupling_v,
    transfer_v,
    ct_v,
    group_s,
    pattern_s,
    weight_v,
    coef_pad,
    coupled_v,
    total_v,
    out_v,
    term_v,
    part_v,
    far_v,
    load_sem,
    near_sem,
    out_sem,
    charge_send,
    charge_recv,
    coef_send,
    coef_recv,
    stage_send,
    stage_recv,
):
    lx, ly = charges.shape[0], charges.shape[1]
    leaves = [(x, y) for x in range(lx) for y in range(ly)]
    rank = basis.shape[2]
    gx = lax.axis_index("gx")
    gy = lax.axis_index("gy")

    def beside(sx, sy):
        return lax.rem(gx + sx + n_gx, n_gx), lax.rem(gy + sy + n_gy, n_gy)

    row_peers = [beside(0, step) for step in range(1, n_gy)]
    column_peers = [beside(step, 0) for step in range(1, n_gx)]
    corners = [beside(sx, sy) for sx, sy in SIDES if sx != 0 and sy != 0]

    barrier = pltpu.get_barrier_semaphore()
    for peer in row_peers + column_peers + corners:
        pl.semaphore_signal(barrier, inc=1, device_id=peer, device_id_type=MESH)

    loads = [
        pltpu.make_async_copy(source, target, load_sem.at[number])
        for number, (source, target) in enumerate(
            [
                (charges, charge_pad.at[pl.ds(1, lx), pl.ds(1, ly)]),
                (basis, basis_v),
                (transfer, transfer_v),
                (coarse_transfer.at[0, 0], ct_v),
                (coarse_group, group_s),
                (coarse_pattern, pattern_s),
                (near_list, near_s),
                (far_list, far_s),
                (coarse_coupling.at[gy], weight_v),
                (coupling, coupling_v),
            ]
        )
    ]
    for load in loads:
        load.start()
    for number, (x, y) in enumerate(leaves):
        pltpu.make_async_copy(near_blocks.at[x, y], near_v.at[number], near_sem.at[number]).start()

    pl.semaphore_wait(barrier, len(row_peers) + len(column_peers) + len(corners))

    charge_copies = []
    for number, (sx, sy) in enumerate(SIDES):
        from_x, to_x = strip(sx, 1, lx)
        from_y, to_y = strip(sy, 1, ly)
        charge_copies.append(
            pltpu.make_async_remote_copy(
                src_ref=charges.at[from_x, from_y],
                dst_ref=charge_pad.at[to_x, to_y],
                send_sem=charge_send.at[number],
                recv_sem=charge_recv.at[number],
                device_id=beside(sx, sy),
                device_id_type=MESH,
            )
        )
    for copy in charge_copies:
        copy.start()

    for load in loads[:4]:
        load.wait()
    cluster = jnp.zeros((out.shape[2], rank), f32)
    for x, y in leaves:
        doubled = jnp.concatenate([basis_v[x, y], basis_v[x, y]], axis=0)
        coef = dot(charge_pad[1 + x, 1 + y], doubled, NT).astype(bf16)
        coef_pad[2 + x, 2 + y] = coef
        cluster += dot(coef[:, :rank], transfer_v[x, y], NT)
    own = ct_v[...]
    term = dot(cluster.astype(bf16), jnp.concatenate([own, own], axis=0), NT).astype(bf16)
    term_v[gy] = term

    def exchange(buffer, slot, peers, stage):
        copies = [
            pltpu.make_async_remote_copy(
                src_ref=buffer.at[slot],
                dst_ref=buffer.at[slot],
                send_sem=stage_send.at[stage],
                recv_sem=stage_recv.at[stage],
                device_id=peer,
                device_id_type=MESH,
            )
            for peer in peers
        ]
        for copy in copies:
            copy.start()

    def all_of(buffer, count, sem):
        view = buffer.at[pl.ds(0, count)]
        pltpu.make_async_copy(view, view, sem).wait()

    exchange(term_v, gy, row_peers, 0)

    coef_copies = []
    for number, (sx, sy) in enumerate(SIDES):
        from_x, to_x = strip(sx, 2, lx)
        from_y, to_y = strip(sy, 2, ly)
        coef_copies.append(
            pltpu.make_async_remote_copy(
                src_ref=coef_pad.at[pl.ds(2 + from_x.start, from_x.size), pl.ds(2 + from_y.start, from_y.size)],
                dst_ref=coef_pad.at[to_x, to_y],
                send_sem=coef_send.at[number],
                recv_sem=coef_recv.at[number],
                device_id=beside(sx, sy),
                device_id_type=MESH,
            )
        )
    for copy in coef_copies:
        copy.start()

    for load in loads[4:]:
        load.wait()
    for copy in charge_copies:
        copy.wait_recv()

    together = 2

    def near_pass(first, last):
        def body(step, carry):
            numbers = [step * together + h for h in range(together)]
            for number in numbers:
                pltpu.make_async_copy(near_v.at[number], near_v.at[number], near_sem.at[number]).wait()
            for number in numbers:
                x, y = number // ly, lax.rem(number, ly)
                total = jnp.zeros((out.shape[2], out.shape[3]), f32)
                for entry in range(near_v.shape[1]):
                    place = near_s[x, y, entry]
                    down = lax.shift_right_logical(place * 11, 5)
                    total += dot(charge_pad[x + down, y + place - 3 * down], near_v[number, entry], NT)
                total_v[number] = total
            return carry

        lax.fori_loop(first // together, last // together, body, 0)

    near_pass(0, 4)

    all_of(term_v, n_gy - 1, stage_recv.at[0])
    lane_half = (lax.broadcasted_iota(jnp.int32, (1, 2 * rank), 1) >= rank).astype(jnp.int32)
    terms = [term_v[slot].astype(f32) for slot in range(n_gy)]
    groups = [group_s[gx * n_gy + slot] for slot in range(n_gy)]
    sums = []
    for pair in range(n_gy // 2):
        total = jnp.zeros((out.shape[2], 2 * rank), f32)
        for slot in range(n_gy):
            total += jnp.where(lane_half == groups[slot] - 2 * pair, terms[slot], 0.0)
        low, high = pattern_s[gy, 2 * pair], pattern_s[gy, 2 * pair + 1]
        allowed = jnp.where(lane_half == 0, low, high) != 0
        sums.append(jnp.where(allowed, total, 0.0).astype(bf16))
    weight = weight_v[...]
    part_v[gx] = dot(jnp.concatenate(sums, axis=1), jnp.concatenate([weight, weight], axis=0), NT)
    exchange(part_v, gx, column_peers, 1)

    near_pass(4, 8)

    for copy in coef_copies:
        copy.wait_recv()
    left_half = lax.broadcasted_iota(jnp.int32, (out.shape[2], 2 * rank), 1) < rank

    def couple(step, carry):
        for h in range(ly):
            x, y = step, h
            picked = []
            for entry in range(far_s.shape[2]):
                place = far_s[x, y, entry]
                offset = jnp.minimum(jnp.maximum(place - 18, 4 * place - 30), place + 3) + 18
                down = lax.shift_right_logical(offset, 3)
                picked.append(coef_pad[x + down, y + offset - 8 * down])
            chosen = [
                jnp.where(left_half, picked[2 * pair].astype(f32), picked[2 * pair + 1].astype(f32)).astype(bf16)
                for pair in range(len(picked) // 2)
            ]
            coupled_v[x, y] = dot(jnp.concatenate(chosen, axis=1), coupling_v[x, y], NT)
        return carry

    lax.fori_loop(0, lx, couple, 0)

    all_of(part_v, n_gx - 1, stage_recv.at[1])
    far_sum = part_v[0]
    for slot in range(1, n_gx):
        far_sum += part_v[slot]
    far_v[gy] = far_sum.astype(bf16)
    exchange(far_v, gy, row_peers, 2)

    near_pass(8, 16)

    all_of(far_v, n_gy - 1, stage_recv.at[2])
    my_group = group_s[gx * n_gy + gy]
    cluster_far = dot(far_v[my_group][:, :rank], own, NN).astype(bf16)

    def finish(step, carry):
        for h in range(ly):
            x, y = step, h
            leaf_far = (coupled_v[x, y] + dot(cluster_far, transfer_v[x, y], NN)).astype(bf16)
            out_v[x, y] = (total_v[x * ly + y] + dot(leaf_far, basis_v[x, y], NN)).astype(bf16)
        return carry

    lax.fori_loop(0, lx, finish, 0)

    store = pltpu.make_async_copy(out_v, out, out_sem)
    store.start()
    all_of(term_v, n_gy - 1, stage_send.at[0])
    all_of(part_v, n_gx - 1, stage_send.at[1])
    all_of(far_v, n_gy - 1, stage_send.at[2])
    for copy in charge_copies + coef_copies:
        copy.wait_send()
    store.wait()


def local(n_gx, n_gy, *arrays):
    charges, basis, near_blocks, near_list, far_list, coupling, transfer, coarse_transfer = arrays[:8]
    coarse_group, coarse_pattern, coarse_coupling = arrays[8:]
    lx, ly, vectors, points = charges.shape
    rank = basis.shape[2]
    halves = 2 * rank
    scratch = [
        pltpu.VMEM((lx + 2, ly + 2, vectors, points), bf16),
        pltpu.VMEM(basis.shape, bf16),
        pltpu.VMEM((lx * ly,) + near_blocks.shape[2:], bf16),
        pltpu.SMEM(near_list.shape, jnp.int32),
        pltpu.SMEM(far_list.shape, jnp.int32),
        pltpu.VMEM(coupling.shape, bf16),
        pltpu.VMEM(transfer.shape, bf16),
        pltpu.VMEM(coarse_transfer.shape[2:], bf16),
        pltpu.SMEM(coarse_group.shape, jnp.int32),
        pltpu.SMEM(coarse_pattern.shape, jnp.int32),
        pltpu.VMEM(coarse_coupling.shape[1:], bf16),
        pltpu.VMEM((lx + 4, ly + 4, vectors, halves), bf16),
        pltpu.VMEM((lx, ly, vectors, rank), f32),
        pltpu.VMEM((lx * ly, vectors, points), f32),
        pltpu.VMEM((lx, ly, vectors, points), bf16),
        pltpu.VMEM((n_gy, vectors, halves), bf16),
        pltpu.VMEM((n_gx, vectors, halves), f32),
        pltpu.VMEM((n_gy, vectors, halves), bf16),
        pltpu.SemaphoreType.DMA((10,)),
        pltpu.SemaphoreType.DMA((lx * ly,)),
        pltpu.SemaphoreType.DMA,
        pltpu.SemaphoreType.DMA((len(SIDES),)),
        pltpu.SemaphoreType.DMA((len(SIDES),)),
        pltpu.SemaphoreType.DMA((len(SIDES),)),
        pltpu.SemaphoreType.DMA((len(SIDES),)),
        pltpu.SemaphoreType.DMA((3,)),
        pltpu.SemaphoreType.DMA((3,)),
    ]
    return pl.pallas_call(
        functools.partial(kernel, n_gx, n_gy),
        out_shape=jax.ShapeDtypeStruct(charges.shape, bf16),
        in_specs=[pl.BlockSpec(memory_space=pltpu.HBM)] * len(arrays),
        out_specs=pl.BlockSpec(memory_space=pl.ANY),
        scratch_shapes=scratch,
        compiler_params=pltpu.CompilerParams(
            collective_id=0, has_side_effects=True, vmem_limit_bytes=60 * 2**20
        ),
    )(*arrays)


def solution(mesh):
    split = P("gx", "gy")
    return jax.shard_map(
        functools.partial(local, mesh.shape["gx"], mesh.shape["gy"]),
        mesh=mesh,
        in_specs=(split,) * 8 + (P(), P(), P()),
        out_specs=split,
        check_vma=False,
    )
```

```python
import functools

import jax
import jax.numpy as jnp
from jax import lax
from jax.experimental import pallas as pl
from jax.experimental.pallas import tpu as pltpu
from jax.sharding import PartitionSpec as P

MESH = pl.DeviceIdType.MESH
NT = (((1,), (1,)), ((), ()))
NN = (((1,), (0,)), ((), ()))
bf16 = jnp.bfloat16
f32 = jnp.float32

SIDES = [(-1, 0), (1, 0), (0, -1), (0, 1), (-1, -1), (-1, 1), (1, -1), (1, 1)]
PAIRS = [
    ((1, 1), (1, 2)),
    ((2, 1), (2, 2)),
    ((3, 1), (3, 2)),
    ((0, 1), (0, 2)),
    ((1, 3), (2, 3)),
    ((1, 0), (2, 0)),
    ((0, 0), (0, 3)),
    ((3, 0), (3, 3)),
]
INNER = 2
COARSE_AT = 4
SPLIT = 4


def dot(left, right, dims):
    return lax.dot_general(left, right, dims, preferred_element_type=f32)


def strip(side, depth, count):
    if side == 0:
        return 0, count, depth
    if side > 0:
        return count - depth, depth, 0
    return 0, depth, count + depth


def choose(step, values):
    chosen = jnp.int32(values[0])
    for number, value in enumerate(values):
        if value != values[0]:
            chosen = jnp.where(step == number, value, chosen)
    return chosen


def kernel(
    n_gx,
    n_gy,
    charges,
    basis,
    near_blocks,
    near_list,
    far_list,
    coupling,
    transfer,
    coarse_transfer,
    coarse_group,
    coarse_pattern,
    coarse_coupling,
    out,
    charge_pad,
    land_x,
    land_y,
    land_corner,
    basis_v,
    near_v,
    near_s,
    far_s,
    coupling_v,
    transfer_v,
    ct_v,
    group_s,
    pattern_s,
    weight_v,
    coef_pad,
    fold_v,
    total_v,
    term_v,
    part_v,
    far_v,
    load_sem,
    near_sem,
    charge_send,
    charge_recv,
    coef_send,
    coef_recv,
    stage_send,
    stage_recv,
):
    lx, ly = charges.shape[0], charges.shape[1]
    vectors, points = charges.shape[2], charges.shape[3]
    leaves = [(x, y) for x in range(lx) for y in range(ly)]
    rank = basis.shape[2]
    gx = lax.axis_index("gx")
    gy = lax.axis_index("gy")

    def beside(sx, sy):
        return lax.rem(gx + sx + n_gx, n_gx), lax.rem(gy + sy + n_gy, n_gy)

    sub_x, sub_y = n_gx // SPLIT, n_gy // SPLIT
    n_plane, n_line = sub_y * SPLIT, sub_x * SPLIT

    def plane_peer(step):
        number = lax.rem(lax.rem(gx, SPLIT) * sub_y + gy // SPLIT + step + n_plane, n_plane)
        return gx // SPLIT * SPLIT + number // sub_y, lax.rem(number, sub_y) * SPLIT + lax.rem(gy, SPLIT)

    def line_peer(step):
        number = lax.rem(gx // SPLIT * SPLIT + lax.rem(gy, SPLIT) + step + n_line, n_line)
        return number // SPLIT * SPLIT + lax.rem(gx, SPLIT), gy // SPLIT * SPLIT + lax.rem(number, SPLIT)

    def group_of(device):
        return group_s[device[0] * n_gy + device[1]]

    plane = [plane_peer(step) for step in range(1, n_plane)]
    line = [line_peer(step) for step in range(1, n_line)]
    around = [beside(sx, sy) for sx, sy in SIDES]

    loads = [
        pltpu.make_async_copy(source, target, load_sem.at[number])
        for number, (source, target) in enumerate(
            [
                (charges, charge_pad.at[pl.ds(1, lx), pl.ds(1, ly)]),
                (basis, basis_v),
                (transfer, transfer_v),
                (coarse_transfer.at[0, 0], ct_v),
                (near_list, near_s),
                (coarse_group, group_s),
                (coarse_pattern, pattern_s),
                (far_list, far_s),
                (coarse_coupling, weight_v),
                (coupling, coupling_v),
            ]
        )
    ]
    order = [leaf for pair in PAIRS for leaf in pair]

    def near_start(first, last):
        for number in range(first, last):
            x, y = order[number]
            pltpu.make_async_copy(near_blocks.at[x, y], near_v.at[number], near_sem.at[number]).start()

    for load in loads[:8]:
        load.start()

    barrier = pltpu.get_barrier_semaphore()
    for peer in plane + line + around:
        pl.semaphore_signal(barrier, inc=1, device_id=peer, device_id_type=MESH)

    for load in loads[:4]:
        load.wait()
    cluster = jnp.zeros((vectors, rank), f32)
    for x, y in leaves:
        doubled = jnp.concatenate([basis_v[x, y], basis_v[x, y]], axis=0)
        coef = dot(charge_pad[1 + x, 1 + y], doubled, NT).astype(bf16)
        coef_pad[2 + x, 2 + y] = coef
        cluster += dot(coef[:, :rank], transfer_v[x, y], NT)
    own = ct_v[...]
    term_v[0] = dot(cluster.astype(bf16), jnp.concatenate([own, own], axis=0), NT).astype(bf16)

    pl.semaphore_wait(barrier, len(plane) + len(line) + len(around))

    def remote(source, target, send, recv, peer):
        return pltpu.make_async_remote_copy(
            src_ref=source, dst_ref=target, send_sem=send, recv_sem=recv, device_id=peer, device_id_type=MESH
        )

    def all_of(buffer, sem):
        view = buffer.at[pl.ds(1, buffer.shape[0] - 1)]
        pltpu.make_async_copy(view, view, sem).wait()

    for step, peer in enumerate(plane, 1):
        remote(term_v.at[0], term_v.at[step], stage_send.at[0], stage_recv.at[0], peer).start()

    charge_copies, coef_copies, landed = [], [], []
    for number, (sx, sy) in enumerate(SIDES):
        at_x, many_x, to_x = strip(sx, 1, lx)
        at_y, many_y, to_y = strip(sy, 1, ly)
        land = land_x.at[number] if number < 2 else land_y.at[number - 2] if number < 4 else land_corner.at[number - 4]
        landed.append((land, many_x, many_y, to_x, to_y))
        charge_copies.append(
            remote(
                charge_pad.at[pl.ds(1 + at_x, many_x), pl.ds(1 + at_y, many_y)],
                land,
                charge_send.at[number],
                charge_recv.at[number],
                beside(sx, sy),
            )
        )
        at_x, many_x, to_x = strip(sx, 2, lx)
        at_y, many_y, to_y = strip(sy, 2, ly)
        coef_copies.append(
            remote(
                coef_pad.at[pl.ds(2 + at_x, many_x), pl.ds(2 + at_y, many_y)],
                coef_pad.at[pl.ds(to_x, many_x), pl.ds(to_y, many_y)],
                coef_send.at[number],
                coef_recv.at[number],
                beside(sx, sy),
            )
        )
    for copy in charge_copies + coef_copies:
        copy.start()

    near_start(0, 2 * INNER)
    loads[8].start()
    near_start(2 * INNER, 8)
    loads[9].start()
    for load in loads[4:8]:
        load.wait()

    def fold(x, carry):
        for y in range(ly):
            down = dot(own, transfer_v[x, y], NN).astype(bf16)
            fold_v[x, y] = dot(down, basis_v[x, y], NN).astype(bf16)
        return carry

    lax.fori_loop(0, lx, fold, 0)

    def take(number):
        charge_copies[number].wait_recv()
        land, many_x, many_y, to_x, to_y = landed[number]
        for x in range(many_x):
            for y in range(many_y):
                charge_pad[to_x + x, to_y + y] = land[x, y]

    def coarse():
        loads[8].wait()
        all_of(term_v, stage_recv.at[0])
        half = (lax.broadcasted_iota(jnp.int32, (1, 2 * rank), 1) >= rank).astype(jnp.int32)
        terms = [term_v[step].astype(f32) for step in range(n_plane)]
        groups = [group_of(plane_peer(-step)) for step in range(n_plane)]
        sums = []
        for pair in range(weight_v.shape[0] // 2):
            total = jnp.zeros((vectors, 2 * rank), f32)
            for step in range(n_plane):
                total += jnp.where(half == groups[step] - 2 * pair, terms[step], 0.0)
            sums.append(total)
        for step in range(n_line):
            group = group_of(line_peer(step))
            allowed = []
            for pair, total in enumerate(sums):
                kept = jnp.where(half == 0, pattern_s[group, 2 * pair], pattern_s[group, 2 * pair + 1]) != 0
                allowed.append(jnp.where(kept, total, 0.0).astype(bf16))
            part = dot(jnp.concatenate(allowed, axis=1), weight_v[group], NT)
            part = jnp.concatenate([part, jnp.zeros_like(part)], axis=1)
            if step == 0:
                far_v[0] = part
            else:
                part_v[step] = part
        for step, peer in enumerate(line, 1):
            remote(part_v.at[step], far_v.at[step], stage_send.at[1], stage_recv.at[1], peer).start()

    def near_leaf(slot, x, y):
        total = jnp.zeros((vectors, points), f32)
        for entry in range(near_v.shape[1]):
            place = near_s[x, y, entry]
            down = lax.shift_right_logical(place * 11, 5)
            total += dot(charge_pad[x + down, y + place - 3 * down], near_v[slot, entry], NT)
        total_v[x, y] = total

    def near(step, carry):
        for number in range(len(SIDES) // 2):
            pl.when(step == INNER + number)(functools.partial(take, number))

        pl.when(step == COARSE_AT)(coarse)

        @pl.when(step == INNER)
        def _():
            near_start(8, len(order))

        slots = [2 * step + h for h in range(2)]
        for slot in slots:
            pltpu.make_async_copy(near_v.at[slot], near_v.at[slot], near_sem.at[slot]).wait()
        for h, slot in enumerate(slots):
            near_leaf(slot, choose(step, [pair[h][0] for pair in PAIRS]), choose(step, [pair[h][1] for pair in PAIRS]))
        return carry

    lax.fori_loop(0, len(PAIRS) - 2, near, 0)
    for number in range(len(SIDES) // 2, len(SIDES)):
        take(number)

    loads[9].wait()
    for copy in coef_copies:
        copy.wait_recv()
    left = lax.broadcasted_iota(jnp.int32, (vectors, 2 * rank), 1) < rank

    def couple(x, carry):
        for y in range(ly):
            picked = []
            for entry in range(far_s.shape[2]):
                place = far_s[x, y, entry]
                offset = jnp.minimum(jnp.maximum(place - 18, 4 * place - 30), place + 3) + 18
                down = lax.shift_right_logical(offset, 3)
                picked.append(coef_pad[x + down, y + offset - 8 * down].astype(f32))
            chosen = [
                jnp.where(left, picked[2 * pair], picked[2 * pair + 1]).astype(bf16) for pair in range(len(picked) // 2)
            ]
            coupled = dot(jnp.concatenate(chosen, axis=1), coupling_v[x, y], NT).astype(bf16)
            total_v[x, y] += dot(coupled, basis_v[x, y], NN)
        return carry

    corner_slots = range(2 * len(PAIRS) - 4, 2 * len(PAIRS))
    for slot in corner_slots:
        pltpu.make_async_copy(near_v.at[slot], near_v.at[slot], near_sem.at[slot]).wait()
    for slot in corner_slots:
        near_leaf(slot, *order[slot])
    for x in range(lx):
        couple(x, 0)

    all_of(far_v, stage_recv.at[1])
    far = far_v[0]
    for step in range(1, n_line):
        far += far_v[step]
    far = far[:, :rank].astype(bf16)
    for x, y in leaves:
        out[x, y] = (total_v[x, y] + dot(far, fold_v[x, y], NN)).astype(bf16)

    all_of(term_v, stage_send.at[0])
    all_of(part_v, stage_send.at[1])
    for copy in charge_copies + coef_copies:
        copy.wait_send()


def local(n_gx, n_gy, *arrays):
    charges, basis, near_blocks, near_list, far_list, coupling, transfer, coarse_transfer = arrays[:8]
    coarse_group, coarse_pattern, coarse_coupling = arrays[8:]
    lx, ly, vectors, points = charges.shape
    halves = 2 * basis.shape[2]
    n_plane, n_line = n_gy // SPLIT * SPLIT, n_gx // SPLIT * SPLIT
    sides = len(SIDES)
    scratch = [
        pltpu.VMEM((lx + 2, ly + 2, vectors, points), bf16),
        pltpu.VMEM((2, 1, ly, vectors, points), bf16),
        pltpu.VMEM((2, lx, 1, vectors, points), bf16),
        pltpu.VMEM((4, 1, 1, vectors, points), bf16),
        pltpu.VMEM(basis.shape, bf16),
        pltpu.VMEM((lx * ly,) + near_blocks.shape[2:], bf16),
        pltpu.SMEM(near_list.shape, jnp.int32),
        pltpu.SMEM(far_list.shape, jnp.int32),
        pltpu.VMEM(coupling.shape, bf16),
        pltpu.VMEM(transfer.shape, bf16),
        pltpu.VMEM(coarse_transfer.shape[2:], bf16),
        pltpu.SMEM(coarse_group.shape, jnp.int32),
        pltpu.SMEM(coarse_pattern.shape, jnp.int32),
        pltpu.VMEM(coarse_coupling.shape, bf16),
        pltpu.VMEM((lx + 4, ly + 4, vectors, halves), bf16),
        pltpu.VMEM(basis.shape, bf16),
        pltpu.VMEM((lx, ly, vectors, points), f32),
        pltpu.VMEM((n_plane, vectors, halves), bf16),
        pltpu.VMEM((n_line, vectors, halves), f32),
        pltpu.VMEM((n_line, vectors, halves), f32),
        pltpu.SemaphoreType.DMA((10,)),
        pltpu.SemaphoreType.DMA((lx * ly,)),
        pltpu.SemaphoreType.DMA((sides,)),
        pltpu.SemaphoreType.DMA((sides,)),
        pltpu.SemaphoreType.DMA((sides,)),
        pltpu.SemaphoreType.DMA((sides,)),
        pltpu.SemaphoreType.DMA((2,)),
        pltpu.SemaphoreType.DMA((2,)),
    ]
    return pl.pallas_call(
        functools.partial(kernel, n_gx, n_gy),
        out_shape=pltpu.VMEM(charges.shape, bf16),
        in_specs=[pl.BlockSpec(memory_space=pl.ANY)] * len(arrays),
        out_specs=pl.BlockSpec(memory_space=pltpu.VMEM),
        scratch_shapes=scratch,
        compiler_params=pltpu.CompilerParams(
            collective_id=0, has_side_effects=True, vmem_limit_bytes=56 * 2**20
        ),
    )(*arrays)


def solution(mesh):
    split = P("gx", "gy")
    return jax.shard_map(
        functools.partial(local, mesh.shape["gx"], mesh.shape["gy"]),
        mesh=mesh,
        in_specs=(split,) * 8 + (P(), P(), P()),
        out_specs=split,
        check_vma=False,
    )
```

```python
import functools

import jax
import jax.numpy as jnp
from jax import lax
from jax.experimental import pallas as pl
from jax.experimental.pallas import tpu as pltpu
from jax.sharding import PartitionSpec as P

MESH = pl.DeviceIdType.MESH
NT = (((1,), (1,)), ((), ()))
NN = (((1,), (0,)), ((), ()))
bf16 = jnp.bfloat16
f32 = jnp.float32

SIDES = [(-1, 0), (1, 0), (0, -1), (0, 1), (-1, -1), (-1, 1), (1, -1), (1, 1)]
PAIRS = [
    ((1, 1), (1, 2)),
    ((2, 1), (2, 2)),
    ((3, 1), (3, 2)),
    ((0, 1), (0, 2)),
    ((1, 3), (2, 3)),
    ((1, 0), (2, 0)),
    ((0, 0), (0, 3)),
    ((3, 0), (3, 3)),
]
INNER = 2
COARSE_AT = 3
SPLIT = 4


def dot(left, right, dims):
    return lax.dot_general(left, right, dims, preferred_element_type=f32)


def strip(side, depth, count):
    if side == 0:
        return 0, count, depth
    if side > 0:
        return count - depth, depth, 0
    return 0, depth, count + depth


def choose(step, values):
    chosen = jnp.int32(values[0])
    for number, value in enumerate(values):
        if value != values[0]:
            chosen = jnp.where(step == number, value, chosen)
    return chosen


def kernel(
    n_gx,
    n_gy,
    charges,
    basis,
    near_blocks,
    near_list,
    far_list,
    coupling,
    transfer,
    coarse_transfer,
    coarse_group,
    coarse_pattern,
    coarse_coupling,
    out,
    charge_v,
    charge_pad,
    land_x,
    land_y,
    land_corner,
    basis_v,
    near_v,
    near_s,
    far_s,
    near_at,
    far_at,
    coupling_v,
    transfer_v,
    ct_v,
    group_s,
    pattern_s,
    weight_v,
    allowed_v,
    coef_v,
    coef_pad,
    coef_x,
    coef_y,
    coef_corner,
    fold_v,
    total_v,
    term_v,
    part_v,
    far_v,
    load_sem,
    near_sem,
    charge_send,
    charge_recv,
    coef_send,
    coef_recv,
    stage_send,
    stage_recv,
):
    lx, ly = charges.shape[0], charges.shape[1]
    vectors, points = charges.shape[2], charges.shape[3]
    leaves = [(x, y) for x in range(lx) for y in range(ly)]
    rank = basis.shape[2]
    gx = lax.axis_index("gx")
    gy = lax.axis_index("gy")

    def beside(sx, sy):
        return lax.rem(gx + sx + n_gx, n_gx), lax.rem(gy + sy + n_gy, n_gy)

    sub_x, sub_y = n_gx // SPLIT, n_gy // SPLIT
    n_plane, n_line = sub_y * SPLIT, sub_x * SPLIT

    def plane_peer(step):
        number = lax.rem(lax.rem(gx, SPLIT) * sub_y + gy // SPLIT + step + n_plane, n_plane)
        return gx // SPLIT * SPLIT + number // sub_y, lax.rem(number, sub_y) * SPLIT + lax.rem(gy, SPLIT)

    def line_peer(step):
        number = lax.rem(gx // SPLIT * SPLIT + lax.rem(gy, SPLIT) + step + n_line, n_line)
        return number // SPLIT * SPLIT + lax.rem(gx, SPLIT), gy // SPLIT * SPLIT + lax.rem(number, SPLIT)

    def group_of(device):
        return group_s[device[0] * n_gy + device[1]]

    def ring(step, size):
        return min(step, size - step)

    plane_steps = sorted(range(1, n_plane), key=lambda step: -ring(step // sub_y, SPLIT) - ring(step % sub_y, sub_y))
    line_steps = sorted(range(1, n_line), key=lambda step: -ring(step, n_line))
    plane = [plane_peer(step) for step in plane_steps]
    line = [line_peer(step) for step in line_steps]
    around = [beside(sx, sy) for sx, sy in SIDES]

    loads = [
        pltpu.make_async_copy(source, target, load_sem.at[number])
        for number, (source, target) in enumerate(
            [
                (charges, charge_v),
                (basis, basis_v),
                (transfer, transfer_v),
                (coarse_transfer.at[0, 0], ct_v),
                (near_list, near_s),
                (coarse_group, group_s),
                (coarse_pattern, pattern_s),
                (far_list, far_s),
                (coarse_coupling, weight_v),
                (coupling, coupling_v),
            ]
        )
    ]
    order = [leaf for pair in PAIRS for leaf in pair]

    def near_start(first, last):
        for number in range(first, last):
            x, y = order[number]
            pltpu.make_async_copy(near_blocks.at[x, y], near_v.at[number], near_sem.at[number]).start()

    for load in loads[:8]:
        load.start()

    barrier = pltpu.get_barrier_semaphore()
    for peer in plane + line + around:
        pl.semaphore_signal(barrier, inc=1, device_id=peer, device_id_type=MESH)

    for load in loads[:4]:
        load.wait()
    cluster = jnp.zeros((vectors, rank), f32)
    for x, y in leaves:
        doubled = jnp.concatenate([basis_v[x, y], basis_v[x, y]], axis=0)
        coef = dot(charge_v[x, y], doubled, NT).astype(bf16)
        coef_v[x, y] = coef
        coef_pad[(2 + x) * (ly + 4) + 2 + y] = coef
        charge_pad[(1 + x) * (ly + 2) + 1 + y] = charge_v[x, y]
        cluster += dot(coef[:, :rank], transfer_v[x, y], NT)
    own = ct_v[...]
    term_v[0] = dot(cluster.astype(bf16), jnp.concatenate([own, own], axis=0), NT).astype(bf16)

    near_start(0, 2 * INNER)
    loads[8].start()
    pl.semaphore_wait(barrier, len(plane) + len(line) + len(around))

    def remote(source, target, send, recv, peer):
        return pltpu.make_async_remote_copy(
            src_ref=source, dst_ref=target, send_sem=send, recv_sem=recv, device_id=peer, device_id_type=MESH
        )

    def all_of(buffer, sem):
        view = buffer.at[pl.ds(1, buffer.shape[0] - 1)]
        pltpu.make_async_copy(view, view, sem).wait()

    for step, peer in zip(plane_steps, plane):
        remote(term_v.at[0], term_v.at[step], stage_send.at[0], stage_recv.at[0], peer).start()

    charge_copies, coef_copies, landed, coef_landed = [], [], [], []
    for number, (sx, sy) in enumerate(SIDES):
        at_x, many_x, to_x = strip(sx, 1, lx)
        at_y, many_y, to_y = strip(sy, 1, ly)
        land = land_x.at[number] if number < 2 else land_y.at[number - 2] if number < 4 else land_corner.at[number - 4]
        landed.append((land, many_x, many_y, to_x, to_y))
        charge_copies.append(
            remote(
                charge_v.at[pl.ds(at_x, many_x), pl.ds(at_y, many_y)],
                land,
                charge_send.at[number],
                charge_recv.at[number],
                beside(sx, sy),
            )
        )
        at_x, many_x, to_x = strip(sx, 2, lx)
        at_y, many_y, to_y = strip(sy, 2, ly)
        land = coef_x.at[number] if number < 2 else coef_y.at[number - 2] if number < 4 else coef_corner.at[number - 4]
        coef_landed.append((land, many_x, many_y, to_x, to_y))
        coef_copies.append(
            remote(
                coef_v.at[pl.ds(at_x, many_x), pl.ds(at_y, many_y)],
                land,
                coef_send.at[number],
                coef_recv.at[number],
                beside(sx, sy),
            )
        )
    for copy in charge_copies + coef_copies:
        copy.start()

    near_start(2 * INNER, 8)
    loads[9].start()
    for load in loads[4:8]:
        load.wait()

    def fold(x, carry):
        for y in range(ly):
            down = dot(own, transfer_v[x, y], NN).astype(bf16)
            fold_v[x, y] = dot(down, basis_v[x, y], NN).astype(bf16)
            for entry in range(near_s.shape[2]):
                place = near_s[x, y, entry]
                near_at[x, y, entry] = x * (ly + 2) + y + place + (ly - 1) * lax.shift_right_logical(place * 11, 5)
            for entry in range(far_s.shape[2]):
                place = far_s[x, y, entry]
                offset = jnp.minimum(jnp.maximum(place - 18, 4 * place - 30), place + 3)
                far_at[x, y, entry] = (x + 2) * (ly + 4) + y + 2 + offset
        return carry

    lax.fori_loop(0, lx, fold, 0)

    half = (lax.broadcasted_iota(jnp.int32, (1, 2 * rank), 1) >= rank).astype(jnp.int32)
    loads[8].wait()
    for step in range(n_line):
        group = group_of(line_peer(step))
        for pair in range(weight_v.shape[0] // 2):
            kept = jnp.where(half == 0, pattern_s[group, 2 * pair], pattern_s[group, 2 * pair + 1]).astype(f32).astype(bf16)
            columns = slice(2 * rank * pair, 2 * rank * (pair + 1))
            allowed_v[step, :, columns] = weight_v[group, :, columns] * kept
    part_v[...] = jnp.zeros_like(part_v)

    def take(number):
        charge_copies[number].wait_recv()
        land, many_x, many_y, to_x, to_y = landed[number]
        for x in range(many_x):
            for y in range(many_y):
                charge_pad[(to_x + x) * (ly + 2) + to_y + y] = land[x, y]

    def coarse():
        all_of(term_v, stage_recv.at[0])
        terms = [term_v[step].astype(f32) for step in range(n_plane)]
        groups = [group_of(plane_peer(-step)) for step in range(n_plane)]
        sums = []
        for pair in range(weight_v.shape[0] // 2):
            total = jnp.zeros((vectors, 2 * rank), f32)
            for step in range(n_plane):
                total += jnp.where(half == groups[step] - 2 * pair, terms[step], 0.0)
            sums.append(total.astype(bf16))
        parts = dot(jnp.concatenate(sums, axis=1), allowed_v[...].reshape(n_line * rank, -1), NT).astype(bf16)
        far_v[0, :, :rank] = parts[:, :rank]
        for step in range(1, n_line):
            part_v[step, :, :rank] = parts[:, step * rank : (step + 1) * rank]
        for step, peer in zip(line_steps, line):
            remote(part_v.at[step], far_v.at[step], stage_send.at[1], stage_recv.at[1], peer).start()

    def near_leaf(slot, x, y):
        total = jnp.zeros((vectors, points), f32)
        for entry in range(near_v.shape[1]):
            total += dot(charge_pad[near_at[x, y, entry]], near_v[slot, entry], NT)
        total_v[x, y] = total

    def near(step, carry):
        @pl.when(step == 1)
        def _():
            near_start(8, len(order))

        for number in range(len(SIDES) // 2):
            pl.when(step == INNER + number)(functools.partial(take, number))

        pl.when(step == COARSE_AT)(coarse)

        slots = [2 * step + h for h in range(2)]
        for slot in slots:
            pltpu.make_async_copy(near_v.at[slot], near_v.at[slot], near_sem.at[slot]).wait()
        for h, slot in enumerate(slots):
            near_leaf(slot, choose(step, [pair[h][0] for pair in PAIRS]), choose(step, [pair[h][1] for pair in PAIRS]))
        return carry

    lax.fori_loop(0, len(PAIRS) - 2, near, 0)
    for number in range(len(SIDES) // 2, len(SIDES)):
        take(number)

    loads[9].wait()
    for copy, (land, many_x, many_y, to_x, to_y) in zip(coef_copies, coef_landed):
        copy.wait_recv()
        for x in range(many_x):
            for y in range(many_y):
                coef_pad[(to_x + x) * (ly + 4) + to_y + y] = land[x, y]
    in_left = (lax.broadcasted_iota(jnp.int32, (vectors, 2 * rank), 1) < rank).astype(f32).astype(bf16)
    in_right = 1 - in_left

    shape = (ly * vectors, ly * rank)
    on_diagonal = lax.broadcasted_iota(jnp.int32, shape, 0) // vectors == lax.broadcasted_iota(jnp.int32, shape, 1) // rank

    def to_points(values, matrices):
        kept = jnp.where(on_diagonal, values, 0.0).astype(bf16)
        return dot(kept, matrices.reshape(ly * rank, points), NN).reshape(ly, vectors, points)

    def couple(x):
        rows = []
        for y in range(ly):
            picked = [coef_pad[far_at[x, y, entry]] for entry in range(far_s.shape[2])]
            chosen = [picked[2 * pair] * in_left + picked[2 * pair + 1] * in_right for pair in range(len(picked) // 2)]
            rows.append(jnp.concatenate(chosen, axis=1))
        coupled = dot(jnp.concatenate(rows, axis=0), coupling_v[x].reshape(ly * rank, -1), NT)
        total_v[x] += to_points(coupled, basis_v[x])

    corner_slots = range(2 * len(PAIRS) - 4, 2 * len(PAIRS))
    for slot in corner_slots:
        pltpu.make_async_copy(near_v.at[slot], near_v.at[slot], near_sem.at[slot]).wait()
    for slot in corner_slots:
        near_leaf(slot, *order[slot])
    for x in range(lx):
        couple(x)

    all_of(far_v, stage_recv.at[1])
    far = far_v[0].astype(f32)
    for step in range(1, n_line):
        far += far_v[step].astype(f32)
    far = jnp.concatenate([far[:, :rank]] * ly, axis=1)
    far = jnp.concatenate([far] * ly, axis=0)
    for x in range(lx):
        out[x] = (total_v[x] + to_points(far, fold_v[x])).astype(bf16)

    all_of(term_v, stage_send.at[0])
    all_of(part_v, stage_send.at[1])
    for copy in charge_copies + coef_copies:
        copy.wait_send()


def local(n_gx, n_gy, *arrays):
    charges, basis, near_blocks, near_list, far_list, coupling, transfer, coarse_transfer = arrays[:8]
    coarse_group, coarse_pattern, coarse_coupling = arrays[8:]
    lx, ly, vectors, points = charges.shape
    halves = 2 * basis.shape[2]
    n_plane, n_line = n_gy // SPLIT * SPLIT, n_gx // SPLIT * SPLIT
    sides = len(SIDES)
    scratch = [
        pltpu.VMEM(charges.shape, bf16),
        pltpu.VMEM(((lx + 2) * (ly + 2), vectors, points), bf16),
        pltpu.VMEM((2, 1, ly, vectors, points), bf16),
        pltpu.VMEM((2, lx, 1, vectors, points), bf16),
        pltpu.VMEM((4, 1, 1, vectors, points), bf16),
        pltpu.VMEM(basis.shape, bf16),
        pltpu.VMEM((lx * ly,) + near_blocks.shape[2:], bf16),
        pltpu.SMEM(near_list.shape, jnp.int32),
        pltpu.SMEM(far_list.shape, jnp.int32),
        pltpu.SMEM(near_list.shape, jnp.int32),
        pltpu.SMEM(far_list.shape, jnp.int32),
        pltpu.VMEM(coupling.shape, bf16),
        pltpu.VMEM(transfer.shape, bf16),
        pltpu.VMEM(coarse_transfer.shape[2:], bf16),
        pltpu.SMEM(coarse_group.shape, jnp.int32),
        pltpu.SMEM(coarse_pattern.shape, jnp.int32),
        pltpu.VMEM(coarse_coupling.shape, bf16),
        pltpu.VMEM((n_line,) + coarse_coupling.shape[1:], bf16),
        pltpu.VMEM((lx, ly, vectors, halves), bf16),
        pltpu.VMEM(((lx + 4) * (ly + 4), vectors, halves), bf16),
        pltpu.VMEM((2, 2, ly, vectors, halves), bf16),
        pltpu.VMEM((2, lx, 2, vectors, halves), bf16),
        pltpu.VMEM((4, 2, 2, vectors, halves), bf16),
        pltpu.VMEM(basis.shape, bf16),
        pltpu.VMEM((lx, ly, vectors, points), f32),
        pltpu.VMEM((n_plane, vectors, halves), bf16),
        pltpu.VMEM((n_line, vectors, halves), bf16),
        pltpu.VMEM((n_line, vectors, halves), bf16),
        pltpu.SemaphoreType.DMA((10,)),
        pltpu.SemaphoreType.DMA((lx * ly,)),
        pltpu.SemaphoreType.DMA((sides,)),
        pltpu.SemaphoreType.DMA((sides,)),
        pltpu.SemaphoreType.DMA((sides,)),
        pltpu.SemaphoreType.DMA((sides,)),
        pltpu.SemaphoreType.DMA((2,)),
        pltpu.SemaphoreType.DMA((2,)),
    ]
    return pl.pallas_call(
        functools.partial(kernel, n_gx, n_gy),
        out_shape=pltpu.VMEM(charges.shape, bf16),
        in_specs=[pl.BlockSpec(memory_space=pl.ANY)] * len(arrays),
        out_specs=pl.BlockSpec(memory_space=pltpu.VMEM),
        scratch_shapes=scratch,
        compiler_params=pltpu.CompilerParams(
            collective_id=0, has_side_effects=True, vmem_limit_bytes=56 * 2**20
        ),
    )(*arrays)


def solution(mesh):
    split = P("gx", "gy")
    return jax.shard_map(
        functools.partial(local, mesh.shape["gx"], mesh.shape["gy"]),
        mesh=mesh,
        in_specs=(split,) * 8 + (P(), P(), P()),
        out_specs=split,
        check_vma=False,
    )
```

```python
import functools

import jax
import jax.numpy as jnp
from jax import lax
from jax.experimental import pallas as pl
from jax.experimental.pallas import tpu as pltpu
from jax.sharding import PartitionSpec as P

MESH = pl.DeviceIdType.MESH
NT = (((1,), (1,)), ((), ()))
NN = (((1,), (0,)), ((), ()))
bf16 = jnp.bfloat16
f32 = jnp.float32

SIDES = [(-1, 0), (1, 0), (0, -1), (0, 1), (-1, -1), (-1, 1), (1, -1), (1, 1)]
PAIRS = [
    ((1, 1), (1, 2)),
    ((2, 1), (2, 2)),
    ((3, 1), (3, 2)),
    ((0, 1), (0, 2)),
    ((1, 3), (2, 3)),
    ((1, 0), (2, 0)),
    ((0, 0), (0, 3)),
    ((3, 0), (3, 3)),
]
INNER = 2
COARSE_AT = 3
SPLIT = 4


def dot(left, right, dims):
    return lax.dot_general(left, right, dims, preferred_element_type=f32)


def strip(side, depth, count):
    if side == 0:
        return 0, count, depth
    if side > 0:
        return count - depth, depth, 0
    return 0, depth, count + depth


def choose(step, values):
    chosen = jnp.int32(values[0])
    for number, value in enumerate(values):
        if value != values[0]:
            chosen = jnp.where(step == number, value, chosen)
    return chosen


def kernel(
    n_gx,
    n_gy,
    charges,
    basis,
    near_blocks,
    near_list,
    far_list,
    coupling,
    transfer,
    coarse_transfer,
    coarse_group,
    coarse_pattern,
    coarse_coupling,
    out,
    charge_v,
    charge_pad,
    land_x,
    land_y,
    land_corner,
    basis_v,
    near_v,
    near_s,
    far_s,
    near_at,
    far_at,
    coupling_v,
    transfer_v,
    ct_v,
    group_s,
    pattern_s,
    weight_v,
    allowed_v,
    coef_v,
    coef_pad,
    coef_x,
    coef_y,
    coef_corner,
    fold_v,
    total_v,
    term_v,
    part_v,
    far_v,
    load_sem,
    near_sem,
    charge_send,
    charge_recv,
    coef_send,
    coef_recv,
    stage_send,
    stage_recv,
):
    lx, ly = charges.shape[0], charges.shape[1]
    vectors, points = charges.shape[2], charges.shape[3]
    leaves = [(x, y) for x in range(lx) for y in range(ly)]
    rank = basis.shape[2]
    gx = lax.axis_index("gx")
    gy = lax.axis_index("gy")

    def beside(sx, sy):
        return lax.rem(gx + sx + n_gx, n_gx), lax.rem(gy + sy + n_gy, n_gy)

    sub_x, sub_y = n_gx // SPLIT, n_gy // SPLIT
    n_plane, n_line = sub_y * SPLIT, sub_x * SPLIT

    def plane_peer(step):
        number = lax.rem(lax.rem(gx, SPLIT) * sub_y + gy // SPLIT + step + n_plane, n_plane)
        return gx // SPLIT * SPLIT + number // sub_y, lax.rem(number, sub_y) * SPLIT + lax.rem(gy, SPLIT)

    def line_peer(step):
        number = lax.rem(gx // SPLIT * SPLIT + lax.rem(gy, SPLIT) + step + n_line, n_line)
        return number // SPLIT * SPLIT + lax.rem(gx, SPLIT), gy // SPLIT * SPLIT + lax.rem(number, SPLIT)

    def group_of(device):
        return group_s[device[0] * n_gy + device[1]]

    def ring(step, size):
        return min(step, size - step)

    plane_steps = sorted(range(1, n_plane), key=lambda step: -ring(step // sub_y, SPLIT) - ring(step % sub_y, sub_y))
    line_steps = sorted(range(1, n_line), key=lambda step: -ring(step, n_line))
    plane = [plane_peer(step) for step in plane_steps]
    line = [line_peer(step) for step in line_steps]
    around = [beside(sx, sy) for sx, sy in SIDES]

    loads = [
        pltpu.make_async_copy(source, target, load_sem.at[number])
        for number, (source, target) in enumerate(
            [
                (charges, charge_v),
                (basis, basis_v),
                (transfer, transfer_v),
                (coarse_transfer.at[0, 0], ct_v),
                (near_list, near_s),
                (coarse_group, group_s),
                (coarse_pattern, pattern_s),
                (far_list, far_s),
                (coarse_coupling, weight_v),
                (coupling, coupling_v),
            ]
        )
    ]
    order = [leaf for pair in PAIRS for leaf in pair]

    def near_start(first, last):
        for number in range(first, last):
            x, y = order[number]
            pltpu.make_async_copy(near_blocks.at[x, y], near_v.at[number], near_sem.at[number]).start()

    for load in loads[:8]:
        load.start()

    barrier = pltpu.get_barrier_semaphore()
    for peer in plane + line + around:
        pl.semaphore_signal(barrier, inc=1, device_id=peer, device_id_type=MESH)

    for load in loads[:4]:
        load.wait()
    cluster = jnp.zeros((vectors, rank), f32)
    in_low = lax.broadcasted_iota(jnp.int32, (vectors, 2 * rank), 1) < rank
    for x, y in leaves:
        if y == 0:
            row = dot(charge_v[x].reshape(ly * vectors, points), basis_v[x].reshape(ly * rank, points), NT)
        both = row[y * vectors : (y + 1) * vectors, y // 2 * 2 * rank : (y // 2 + 1) * 2 * rank]
        swapped = jnp.concatenate([both[:, rank:], both[:, :rank]], axis=1)
        coef = jnp.where(in_low, swapped, both) if y % 2 else jnp.where(in_low, both, swapped)
        coef = coef.astype(bf16)
        coef_v[x, y] = coef
        coef_pad[(2 + x) * (ly + 4) + 2 + y] = coef
        charge_pad[(1 + x) * (ly + 2) + 1 + y] = charge_v[x, y]
        cluster += dot(coef[:, :rank], transfer_v[x, y], NT)
    own = ct_v[...]
    term_v[0] = dot(cluster.astype(bf16), jnp.concatenate([own, own], axis=0), NT).astype(bf16)

    loads[8].start()
    near_start(0, 2 * INNER)
    pl.semaphore_wait(barrier, len(plane) + len(line) + len(around))

    def remote(source, target, send, recv, peer):
        return pltpu.make_async_remote_copy(
            src_ref=source, dst_ref=target, send_sem=send, recv_sem=recv, device_id=peer, device_id_type=MESH
        )

    def all_of(buffer, sem):
        view = buffer.at[pl.ds(1, buffer.shape[0] - 1)]
        pltpu.make_async_copy(view, view, sem).wait()

    for step, peer in zip(plane_steps, plane):
        remote(term_v.at[0], term_v.at[step], stage_send.at[0], stage_recv.at[0], peer).start()

    charge_copies, coef_copies, landed, coef_landed = [], [], [], []
    for number, (sx, sy) in enumerate(SIDES):
        at_x, many_x, to_x = strip(sx, 1, lx)
        at_y, many_y, to_y = strip(sy, 1, ly)
        land = land_x.at[number] if number < 2 else land_y.at[number - 2] if number < 4 else land_corner.at[number - 4]
        landed.append((land, many_x, many_y, to_x, to_y))
        charge_copies.append(
            remote(
                charge_v.at[pl.ds(at_x, many_x), pl.ds(at_y, many_y)],
                land,
                charge_send.at[number],
                charge_recv.at[number],
                beside(sx, sy),
            )
        )
        at_x, many_x, to_x = strip(sx, 2, lx)
        at_y, many_y, to_y = strip(sy, 2, ly)
        land = coef_x.at[number] if number < 2 else coef_y.at[number - 2] if number < 4 else coef_corner.at[number - 4]
        coef_landed.append((land, many_x, many_y, to_x, to_y))
        coef_copies.append(
            remote(
                coef_v.at[pl.ds(at_x, many_x), pl.ds(at_y, many_y)],
                land,
                coef_send.at[number],
                coef_recv.at[number],
                beside(sx, sy),
            )
        )
    for copy in charge_copies + coef_copies:
        copy.start()

    near_start(2 * INNER, 8)
    loads[9].start()
    for load in loads[4:8]:
        load.wait()

    def fold(x, carry):
        for y in range(ly):
            down = dot(own, transfer_v[x, y], NN).astype(bf16)
            fold_v[x, y] = dot(down, basis_v[x, y], NN).astype(bf16)
            for entry in range(near_s.shape[2]):
                place = near_s[x, y, entry]
                near_at[x, y, entry] = x * (ly + 2) + y + place + (ly - 1) * lax.shift_right_logical(place * 11, 5)
            for entry in range(far_s.shape[2]):
                place = far_s[x, y, entry]
                offset = jnp.minimum(jnp.maximum(place - 18, 4 * place - 30), place + 3)
                far_at[x, y, entry] = (x + 2) * (ly + 4) + y + 2 + offset
        return carry

    lax.fori_loop(0, lx, fold, 0)

    half = (lax.broadcasted_iota(jnp.int32, (1, 2 * rank), 1) >= rank).astype(jnp.int32)
    loads[8].wait()
    for step in range(n_line):
        group = group_of(line_peer(step))
        for pair in range(weight_v.shape[0] // 2):
            kept = jnp.where(half == 0, pattern_s[group, 2 * pair], pattern_s[group, 2 * pair + 1]).astype(f32).astype(bf16)
            columns = slice(2 * rank * pair, 2 * rank * (pair + 1))
            allowed_v[step, :, columns] = weight_v[group, :, columns] * kept
    part_v[...] = jnp.zeros_like(part_v)

    def take(number):
        charge_copies[number].wait_recv()
        land, many_x, many_y, to_x, to_y = landed[number]
        for x in range(many_x):
            for y in range(many_y):
                charge_pad[(to_x + x) * (ly + 2) + to_y + y] = land[x, y]

    def coarse():
        all_of(term_v, stage_recv.at[0])
        terms = [term_v[step].astype(f32) for step in range(n_plane)]
        groups = [group_of(plane_peer(-step)) for step in range(n_plane)]
        sums = []
        for pair in range(weight_v.shape[0] // 2):
            total = jnp.zeros((vectors, 2 * rank), f32)
            for step in range(n_plane):
                total += jnp.where(half == groups[step] - 2 * pair, terms[step], 0.0)
            sums.append(total.astype(bf16))
        parts = dot(jnp.concatenate(sums, axis=1), allowed_v[...].reshape(n_line * rank, -1), NT).astype(bf16)
        far_v[0, :, :rank] = parts[:, :rank]
        for step in range(1, n_line):
            part_v[step, :, :rank] = parts[:, step * rank : (step + 1) * rank]
        for step, peer in zip(line_steps, line):
            remote(part_v.at[step], far_v.at[step], stage_send.at[1], stage_recv.at[1], peer).start()

    def near_leaf(slot, x, y):
        total = jnp.zeros((vectors, points), f32)
        for entry in range(near_v.shape[1]):
            total += dot(charge_pad[near_at[x, y, entry]], near_v[slot, entry], NT)
        total_v[x, y] = total

    def near(step, carry):
        @pl.when(step == 1)
        def _():
            near_start(8, len(order))

        for number in range(len(SIDES) // 2):
            pl.when(step == INNER + number)(functools.partial(take, number))

        pl.when(step == COARSE_AT)(coarse)

        slots = [2 * step + h for h in range(2)]
        for slot in slots:
            pltpu.make_async_copy(near_v.at[slot], near_v.at[slot], near_sem.at[slot]).wait()
        for h, slot in enumerate(slots):
            near_leaf(slot, choose(step, [pair[h][0] for pair in PAIRS]), choose(step, [pair[h][1] for pair in PAIRS]))
        return carry

    lax.fori_loop(0, len(PAIRS) - 2, near, 0)
    for number in range(len(SIDES) // 2, len(SIDES)):
        take(number)

    loads[9].wait()
    for copy, (land, many_x, many_y, to_x, to_y) in zip(coef_copies, coef_landed):
        copy.wait_recv()
        for x in range(many_x):
            for y in range(many_y):
                coef_pad[(to_x + x) * (ly + 4) + to_y + y] = land[x, y]
    in_left = (lax.broadcasted_iota(jnp.int32, (vectors, 2 * rank), 1) < rank).astype(f32).astype(bf16)
    in_right = 1 - in_left

    shape = (ly * vectors, ly * rank)
    on_diagonal = lax.broadcasted_iota(jnp.int32, shape, 0) // vectors == lax.broadcasted_iota(jnp.int32, shape, 1) // rank

    def to_points(values, matrices):
        kept = jnp.where(on_diagonal, values, 0.0).astype(bf16)
        return dot(kept, matrices.reshape(ly * rank, points), NN).reshape(ly, vectors, points)

    def couple(x):
        rows = []
        for y in range(ly):
            picked = [coef_pad[far_at[x, y, entry]] for entry in range(far_s.shape[2])]
            chosen = [picked[2 * pair] * in_left + picked[2 * pair + 1] * in_right for pair in range(len(picked) // 2)]
            rows.append(jnp.concatenate(chosen, axis=1))
        coupled = dot(jnp.concatenate(rows, axis=0), coupling_v[x].reshape(ly * rank, -1), NT)
        total_v[x] += to_points(coupled, basis_v[x])

    corner_slots = range(2 * len(PAIRS) - 4, 2 * len(PAIRS))
    for slot in corner_slots:
        pltpu.make_async_copy(near_v.at[slot], near_v.at[slot], near_sem.at[slot]).wait()
    for slot in corner_slots:
        near_leaf(slot, *order[slot])
    for x in range(lx):
        couple(x)

    all_of(far_v, stage_recv.at[1])
    far = far_v[0].astype(f32)
    for step in range(1, n_line):
        far += far_v[step].astype(f32)
    far = jnp.concatenate([far[:, :rank]] * ly, axis=1)
    far = jnp.concatenate([far] * ly, axis=0)
    for x in range(lx):
        out[x] = (total_v[x] + to_points(far, fold_v[x])).astype(bf16)

    all_of(term_v, stage_send.at[0])
    all_of(part_v, stage_send.at[1])
    for copy in charge_copies + coef_copies:
        copy.wait_send()


def local(n_gx, n_gy, *arrays):
    charges, basis, near_blocks, near_list, far_list, coupling, transfer, coarse_transfer = arrays[:8]
    coarse_group, coarse_pattern, coarse_coupling = arrays[8:]
    lx, ly, vectors, points = charges.shape
    halves = 2 * basis.shape[2]
    n_plane, n_line = n_gy // SPLIT * SPLIT, n_gx // SPLIT * SPLIT
    sides = len(SIDES)
    scratch = [
        pltpu.VMEM(charges.shape, bf16),
        pltpu.VMEM(((lx + 2) * (ly + 2), vectors, points), bf16),
        pltpu.VMEM((2, 1, ly, vectors, points), bf16),
        pltpu.VMEM((2, lx, 1, vectors, points), bf16),
        pltpu.VMEM((4, 1, 1, vectors, points), bf16),
        pltpu.VMEM(basis.shape, bf16),
        pltpu.VMEM((lx * ly,) + near_blocks.shape[2:], bf16),
        pltpu.SMEM(near_list.shape, jnp.int32),
        pltpu.SMEM(far_list.shape, jnp.int32),
        pltpu.SMEM(near_list.shape, jnp.int32),
        pltpu.SMEM(far_list.shape, jnp.int32),
        pltpu.VMEM(coupling.shape, bf16),
        pltpu.VMEM(transfer.shape, bf16),
        pltpu.VMEM(coarse_transfer.shape[2:], bf16),
        pltpu.SMEM(coarse_group.shape, jnp.int32),
        pltpu.SMEM(coarse_pattern.shape, jnp.int32),
        pltpu.VMEM(coarse_coupling.shape, bf16),
        pltpu.VMEM((n_line,) + coarse_coupling.shape[1:], bf16),
        pltpu.VMEM((lx, ly, vectors, halves), bf16),
        pltpu.VMEM(((lx + 4) * (ly + 4), vectors, halves), bf16),
        pltpu.VMEM((2, 2, ly, vectors, halves), bf16),
        pltpu.VMEM((2, lx, 2, vectors, halves), bf16),
        pltpu.VMEM((4, 2, 2, vectors, halves), bf16),
        pltpu.VMEM(basis.shape, bf16),
        pltpu.VMEM((lx, ly, vectors, points), f32),
        pltpu.VMEM((n_plane, vectors, halves), bf16),
        pltpu.VMEM((n_line, vectors, halves), bf16),
        pltpu.VMEM((n_line, vectors, halves), bf16),
        pltpu.SemaphoreType.DMA((10,)),
        pltpu.SemaphoreType.DMA((lx * ly,)),
        pltpu.SemaphoreType.DMA((sides,)),
        pltpu.SemaphoreType.DMA((sides,)),
        pltpu.SemaphoreType.DMA((sides,)),
        pltpu.SemaphoreType.DMA((sides,)),
        pltpu.SemaphoreType.DMA((2,)),
        pltpu.SemaphoreType.DMA((2,)),
    ]
    return pl.pallas_call(
        functools.partial(kernel, n_gx, n_gy),
        out_shape=pltpu.VMEM(charges.shape, bf16),
        in_specs=[pl.BlockSpec(memory_space=pl.ANY)] * len(arrays),
        out_specs=pl.BlockSpec(memory_space=pltpu.VMEM),
        scratch_shapes=scratch,
        compiler_params=pltpu.CompilerParams(
            collective_id=0, has_side_effects=True, vmem_limit_bytes=56 * 2**20
        ),
    )(*arrays)


def solution(mesh):
    split = P("gx", "gy")
    return jax.shard_map(
        functools.partial(local, mesh.shape["gx"], mesh.shape["gy"]),
        mesh=mesh,
        in_specs=(split,) * 8 + (P(), P(), P()),
        out_specs=split,
        check_vma=False,
    )
```
